512 devices in a mesh: tm: 16 (over z_lo, x), ctx: 32 (over y, z_hi, core).
Axes of the slice: x: 4, y: 4, z: 16 (z_hi: 4, z_lo: 4; z = z_hi * 4 + z_lo), core: 2. Of those that a mesh axis runs over, the one named last changes fastest.
Arguments:
- states: float32 [16, 3072, 64], P('tm', 'ctx'), may hold values from -6 to 6
- noise_draws: float32 [16, 3072, 64], P('tm', 'ctx'), may hold values from -6 to 6
- plan: int32 [17], replicated, may hold values from 0 to 1000, as said below
- w_embed: bfloat16 [64, 3072], replicated, may hold values from -0.75 to 0.75
- w_time: bfloat16 [128, 3072], replicated, may hold values from -0.5 to 0.5
- w_query: bfloat16 [16, 3072, 128], P('tm'), may hold values from -0.109375 to 0.109375
- w_key: bfloat16 [16, 3072, 128], P('tm'), may hold values from -0.109375 to 0.109375
- w_value: bfloat16 [16, 3072, 128], P('tm'), may hold values from -0.109375 to 0.109375
- gain_query: float32 [16, 128], P('tm'), may hold values from 0.5 to 16, as said below
- gain_key: float32 [16, 128], P('tm'), may hold values from 0.5 to 16, as said below
- w_out: bfloat16 [16, 128, 3072], P('tm'), may hold values from -0.5 to 0.5
- w_final: bfloat16 [3072, 64], replicated, may hold values from -0.109375 to 0.109375
Outputs:
- new_states: float32 [16, 3072, 64], P('tm', 'ctx')
The draws below stay inside these ranges and needn't reach their ends.
Inputs may be any that keep to these rules, and one draw needn't show every extreme that they name: plan[0] is 1000 and each later entry is smaller than the one before by 31 to 61. `gain_query`: positive gains. `gain_key`: positive gains.
All inputs are finite; a program needn't handle non-finite values.
Results may differ from the reference program's by a relative error of at most 0.014.
The reference program's roundings to bfloat16 on the way count: a program that leaves them out, or rounds other values in their place, can miss the bound.
Values may be sent and summed in bfloat16 or wider, within the bound.
No kernel may reach another device: no remote copies, remote signals or barrier semaphores. Data moves between devices by JAX's collectives and lax.ppermute only.
A program may use at most 64 MiB of HBM per device.

```python
import math
import jax
import jax.numpy as jnp
from jax import lax

D = 3072
HEAD_DIM = 128
CHAN = 64
FREQ = 128
HEADS = 16
TSTEPS = 16
TILE = 96
KEY_TILES = 3
TOKENS = 3072
TILES = 32


def draw_plan(key, part):
    gaps = jax.random.randint(key, (TSTEPS,), 500 // TSTEPS, 1000 // TSTEPS)
    falls = jnp.concatenate([jnp.zeros((1,), jnp.int32), jnp.cumsum(gaps).astype(jnp.int32)])
    return (1000 - falls).astype(jnp.int32)


def gain_table(key, salt):
    own_key = jax.random.fold_in(key, salt)
    key_a = jax.random.fold_in(own_key, 0)
    base = jnp.exp(jax.random.uniform(key_a, (HEADS, HEAD_DIM), jnp.float32, math.log(0.5), math.log(2.0)))
    return base


def draw_gain_query(key, part):
    return gain_table(key, 11)


def draw_gain_key(key, part):
    return gain_table(key, 12)


def block_levels(rng, shape, pieces, low, high):
    def one(position, shards_of):
        heights = jax.random.uniform(jax.random.fold_in(jax.random.fold_in(rng, 6), position), (shards_of,), jnp.float32, low / len(pieces), high / len(pieces))
        return jnp.repeat(jnp.exp(heights), shape[position] // shards_of).reshape((-1,) + (1,) * (len(shape) - position - 1))

    loudness = one(*pieces[0])
    for cut in pieces[1:]:
        loudness = loudness * one(*cut)
    return loudness


def bell_draw(rng, dims, scale, bound, shards=(), kind=jnp.bfloat16):
    result = jax.random.normal(rng, dims, jnp.float32) * scale
    if len(shards) > 0:
        result = block_levels(rng, dims, shards, -0.22, 0.18) * result
    return jnp.clip(result, min=-bound, max=bound).astype(kind)


def setup_inputs(seed: int = 0) -> dict:
    arg_keys = jax.random.split(jax.random.key(seed), 13)
    return {
        "states": bell_draw(arg_keys[0], (TSTEPS, TOKENS, CHAN), 1.0, 6.0, ((0, 16), (1, 32)), jnp.float32),
        "noise_draws": bell_draw(arg_keys[1], (TSTEPS, TOKENS, CHAN), 1.0, 6.0, ((0, 16), (1, 32)), jnp.float32),
        "plan": draw_plan(jax.random.fold_in(arg_keys[12], 71), 0),
        "w_embed": bell_draw(arg_keys[3], (CHAN, D), CHAN ** -0.5, 0.75),
        "w_time": bell_draw(arg_keys[4], (FREQ, D), FREQ ** -0.5, 0.5),
        "w_query": bell_draw(arg_keys[5], (HEADS, D, HEAD_DIM), D ** -0.5, 0.109375, ((0, 16),)),
        "w_key": bell_draw(arg_keys[6], (HEADS, D, HEAD_DIM), D ** -0.5, 0.109375, ((0, 16),)),
        "w_value": bell_draw(arg_keys[7], (HEADS, D, HEAD_DIM), D ** -0.5, 0.109375, ((0, 16),)),
        "gain_query": draw_gain_query(jax.random.fold_in(arg_keys[12], 71), 0),
        "gain_key": draw_gain_key(jax.random.fold_in(arg_keys[12], 71), 0),
        "w_out": bell_draw(arg_keys[10], (HEADS, HEAD_DIM, D), HEAD_DIM ** -0.5, 0.5, ((0, 16),)),
        "w_final": bell_draw(arg_keys[11], (D, CHAN), D ** -0.5, 0.109375),
    }


def fourier_rows(plan):
    half_freq = FREQ // 2
    frequency = jnp.exp(-math.log(10000.0) * jnp.arange(half_freq, dtype=jnp.float32) / half_freq)
    phase_arg = plan[:TSTEPS].astype(jnp.float32)[:, None] * frequency[None, :]
    return jnp.concatenate([jnp.cos(phase_arg), jnp.sin(phase_arg)], axis=1).astype(jnp.bfloat16)

def rms_gain(values_in, gain_row):
    scale = lax.rsqrt(lax.optimization_barrier(jnp.mean(values_in * values_in, axis=-1, keepdims=True)) + 1e-06)
    return values_in * scale * gain_row

def window_rows(rows):
    tiled = rows.reshape(TSTEPS, TILES, TILE, HEAD_DIM)
    padded = jnp.pad(tiled, ((0, 0), (1, 1), (0, 0), (0, 0)))
    joined = jnp.concatenate([padded[:, :-2], padded[:, 1:-1], padded[:, 2:]], axis=2)
    return joined.astype(jnp.float32)

def reference(states, noise_draws, plan, w_embed, w_time, w_query, w_key, w_value, gain_query, gain_key, w_out, w_final):
    features = fourier_rows(plan)
    time_shift = jnp.dot(features, w_time, preferred_element_type=jnp.float32)
    latents = states.astype(jnp.bfloat16)
    embedded = jnp.dot(latents.reshape(TSTEPS * TOKENS, CHAN), w_embed, preferred_element_type=jnp.float32)
    hidden = (embedded.reshape(TSTEPS, TOKENS, D) + time_shift[:, None, :]).astype(jnp.bfloat16)
    flat_hidden = hidden.reshape(TSTEPS * TOKENS, D)
    tile_ids = jnp.arange(TILES, dtype=jnp.int32)
    block_of = jnp.arange(KEY_TILES * TILE, dtype=jnp.int32) // TILE
    valid = (block_of[None, :] == 1) | (block_of[None, :] == 0) & (tile_ids[:, None] > 0) | (block_of[None, :] == 2) & (tile_ids[:, None] < TILES - 1)
    valid = valid[None, :, None, :]

    def one_head(operands):
        query_w, key_w, value_w, query_gain, key_gain, out_w = operands
        queries = rms_gain(jnp.dot(flat_hidden, query_w, preferred_element_type=jnp.float32), query_gain).astype(jnp.bfloat16)
        key_rows = rms_gain(jnp.dot(flat_hidden, key_w, preferred_element_type=jnp.float32), key_gain).astype(jnp.bfloat16)
        value_rows = jnp.dot(flat_hidden, value_w, preferred_element_type=jnp.float32).astype(jnp.bfloat16)
        query_tiles = queries.reshape(TSTEPS, TILES, TILE, HEAD_DIM).astype(jnp.float32)
        key_sel = window_rows(key_rows)
        value_sel = window_rows(value_rows)
        scores = jnp.einsum('sgqe,sgke->sgqk', query_tiles, key_sel) / math.sqrt(HEAD_DIM)
        top_score = lax.optimization_barrier(jnp.max(jnp.where(valid, scores, -1e+30), axis=-1, keepdims=True))
        expo = jnp.where(valid, jnp.exp(scores - top_score), 0.0)
        attn_probs = (expo / lax.optimization_barrier(jnp.sum(expo, axis=-1, keepdims=True))).astype(jnp.bfloat16)
        attended = jnp.einsum('sgqk,sgke->sgqe', attn_probs.astype(jnp.float32), value_sel).astype(jnp.bfloat16)
        projected = jnp.dot(attended.reshape(TSTEPS * TOKENS, HEAD_DIM), out_w, preferred_element_type=jnp.float32).astype(jnp.bfloat16)
        return jnp.dot(projected, w_final, preferred_element_type=jnp.float32)
    head_terms = lax.map(one_head, (w_query, w_key, w_value, gain_query, gain_key, w_out))
    drift_rows = lax.optimization_barrier(jnp.sum(head_terms, axis=0)) + jnp.dot(flat_hidden, w_final, preferred_element_type=jnp.float32)
    drift_rows = drift_rows.reshape(TSTEPS, TOKENS, CHAN)
    step_sizes = (plan[:-1] - plan[1:]).astype(jnp.float32) / 1000.0
    increment = step_sizes[:, None, None] * drift_rows + jnp.sqrt(step_sizes)[:, None, None] * noise_draws
    return states[0][None, :, :] + jnp.cumsum(increment, axis=0)
```

```python
import functools
import math

import jax
import jax.numpy as jnp
from jax import lax
from jax.experimental import pallas as pl
from jax.experimental.pallas import tpu as pltpu
from jax.sharding import PartitionSpec as P

F32, BF16 = jnp.float32, jnp.bfloat16
MIB = 1 << 20
VMEM = pl.BlockSpec(memory_space=pltpu.VMEM)
ANY = pl.BlockSpec(memory_space=pl.ANY)
SMEM = pl.BlockSpec(memory_space=pltpu.SMEM)
NT = (((1,), (1,)), ((), ()))


def fourier_rows(plan, freq_count, step_count):
    half_freq = freq_count // 2
    frequency = jnp.exp(-math.log(10000.0) * jnp.arange(half_freq, dtype=F32) / half_freq)
    phase_arg = plan[:step_count].astype(F32)[:, None] * frequency[None, :]
    return jnp.concatenate([jnp.cos(phase_arg), jnp.sin(phase_arg)], axis=1).astype(BF16)


def dot(a, b):
    return jnp.dot(a, b, preferred_element_type=F32)


def split(value):
    high = value.astype(BF16)
    return high, (value - high.astype(F32)).astype(BF16)


def pack_kernel(state_ref, copies_ref):
    rows = state_ref[...].T.astype(BF16)
    half = rows.shape[0] // 2
    packed = jnp.concatenate([rows[:half], rows[half:]], axis=1)
    copies_ref[...] = jnp.broadcast_to(packed[None], copies_ref.shape)


def fold_kernel(embed_ref, time_ref, value_ref, out_ref, final_ref, into_value, into_final, tail):
    freq, width = time_ref.shape[0], value_ref.shape[1]
    channels = final_ref.shape[0]
    final = final_ref[...]
    for rows, ref in (((0, freq), time_ref), ((freq, freq + embed_ref.shape[0]), embed_ref)):
        left = ref[...]
        high, low = split(dot(left, value_ref[...]))
        into_value[rows[0] : rows[1], :width] = high
        into_value[rows[0] : rows[1], width:] = low
        product = lax.dot_general(left, final, NT, preferred_element_type=F32)
        into_final[rows[0] : rows[1], :] = jnp.concatenate(split(product), axis=1)
    product = lax.dot_general(out_ref[...], final, NT, preferred_element_type=F32)
    tail[...] = jnp.concatenate(split(product), axis=1)


def rms_gain(values, gain):
    scale = lax.rsqrt(jnp.mean(values * values, axis=-1, keepdims=True) + 1e-06)
    return values * scale * gain


def fill_inputs(latent_ref, feature_ref, inputs):
    steps, half, both = latent_ref.shape
    channels, freq = both // 2, feature_ref.shape[1]
    for s in range(steps):
        row = s * 2 * half
        packed = latent_ref[s]
        inputs[row : row + half, freq:] = packed[:, :channels]
        inputs[row + half : row + 2 * half, freq:] = packed[:, channels:]
        inputs[row : row + 2 * half, :freq] = jnp.broadcast_to(
            feature_ref[s : s + 1, :], (2 * half, freq)
        )


def project_kernel(
    own,
    block,
    chunk,
    latent_ref,
    feature_ref,
    embed_ref,
    time_ref,
    left_ref,
    right_ref,
    *rest,
):
    if own:
        into_value, gain_query, gain_key, query_out, pair_out = rest[:5]
    else:
        gain_key, pair_out = rest[:2]
    inputs, first, second, sems = rest[-4:]
    freq, width = time_ref.shape[0], left_ref.shape[1]
    copies = [
        pltpu.make_async_copy(time_ref, first.at[:freq], sems.at[0]),
        pltpu.make_async_copy(embed_ref, first.at[freq:], sems.at[1]),
        pltpu.make_async_copy(left_ref, second.at[:, :width], sems.at[2]),
        pltpu.make_async_copy(right_ref, second.at[:, width:], sems.at[3]),
    ]
    for copy in copies:
        copy.start()
    fill_inputs(latent_ref, feature_ref, inputs)
    for copy in copies:
        copy.wait()
    rows, depth = inputs.shape[0], first.shape[1]

    def step(i, carry):
        here = pl.ds(pl.multiple_of(i * block, block), block)
        taken = inputs[here, :]
        total = None
        for n in range(0, depth, chunk):
            hidden = dot(taken, first[:, n : n + chunk]).astype(BF16)
            part = dot(hidden, second[n : n + chunk, :])
            total = part if total is None else total + part
        if own:
            query_out[here, :] = rms_gain(total[:, :width], gain_query[...]).astype(BF16)
            pair_out[here, :width] = rms_gain(total[:, width:], gain_key[...]).astype(BF16)
            values = dot(taken, into_value[...])
            pair_out[here, width:] = (values[:, :width] + values[:, width:]).astype(BF16)
        else:
            pair_out[here, :width] = rms_gain(total[:, :width], gain_key[...]).astype(BF16)
            pair_out[here, width:] = total[:, width:].astype(BF16)
        return carry

    lax.fori_loop(0, rows // block, step, 0)


def attend_kernel(
    plan_ref,
    query_ref,
    own_ref,
    inner_ref,
    outer_ref,
    tail_ref,
    latent_ref,
    feature_ref,
    into_final,
    state_ref,
    noise_ref,
    sent_ref,
):
    steps, half, both = sent_ref.shape
    channels, tile = both // 2, 2 * half
    width = query_ref.shape[1]
    mine, place = lax.axis_index("tm"), lax.axis_index("ctx")
    alone = (place == 0) | (place == lax.axis_size("ctx") - 1)
    scale = 1.0 / math.sqrt(width)

    def size_of(s):
        return (plan_ref[s] - plan_ref[s + 1]).astype(F32) / 1000.0

    own_size = jnp.full((tile, channels), size_of(mine), F32)
    packed = latent_ref[mine]
    rows = jnp.concatenate([packed[:, :channels], packed[:, channels:]], axis=0)
    features = feature_ref[...].astype(F32)
    chosen = lax.broadcasted_iota(jnp.int32, features.shape, 0) == mine
    features = jnp.sum(jnp.where(chosen, features, 0.0), axis=0, keepdims=True).astype(BF16)
    features = jnp.broadcast_to(features, (tile, features.shape[1]))
    taken = jnp.concatenate([features, rows], axis=1)
    residual = dot(taken, into_final[...])
    extra = own_size * (residual[:, :channels] + residual[:, channels:])
    extra = extra + jnp.sqrt(own_size) * noise_ref[...].T
    extra = extra + jnp.where(mine == 0, state_ref[...].T, 0.0)
    column = lax.broadcasted_iota(jnp.int32, (tile, 3 * tile), 1)
    hidden_key = (column >= 2 * tile) & alone

    running = jnp.zeros((tile, channels), F32)
    for s in range(steps):
        here = slice(s * tile, (s + 1) * tile)
        keys = jnp.concatenate([r[here, :width] for r in (own_ref, inner_ref, outer_ref)], axis=0)
        values = jnp.concatenate([r[here, width:] for r in (own_ref, inner_ref, outer_ref)], axis=0)
        scores = lax.dot_general(query_ref[here, :], keys, NT, preferred_element_type=F32) * scale
        scores = jnp.where(hidden_key, -1e30, scores)
        expo = jnp.exp(scores - jnp.max(scores, axis=-1, keepdims=True))
        probs = (expo * (1.0 / jnp.sum(expo, axis=-1, keepdims=True))).astype(BF16)
        attended = dot(probs, values).astype(BF16)
        terms = dot(attended, tail_ref[...])
        running = running + size_of(s) * (terms[:, :channels] + terms[:, channels:])
        total = running + jnp.where(s >= mine, extra, 0.0)
        sent_ref[s] = jnp.concatenate([total[:half], total[half:]], axis=1).astype(BF16)


def sum_kernel(taken_ref, out_ref):
    total = jnp.sum(taken_ref[...].astype(F32), axis=0)
    channels = total.shape[1] // 2
    out_ref[...] = jnp.concatenate([total[:, :channels], total[:, channels:]], axis=0).T


def call(kernel, shapes, specs, scratch=(), limit=24, flops=0, moved=0):
    many = isinstance(shapes, (list, tuple))
    return pl.pallas_call(
        kernel,
        out_shape=shapes,
        in_specs=specs,
        out_specs=[VMEM] * len(shapes) if many else VMEM,
        scratch_shapes=list(scratch),
        compiler_params=pltpu.CompilerParams(vmem_limit_bytes=limit * MIB),
        cost_estimate=pl.CostEstimate(flops=flops, bytes_accessed=moved, transcendentals=0),
    )


def struct(shape, dtype):
    return jax.ShapeDtypeStruct(shape, dtype)


def per_device(
    states,
    noise_draws,
    plan,
    w_embed,
    w_time,
    w_query,
    w_key,
    w_value,
    gain_query,
    gain_key,
    w_out,
    w_final,
):
    steps = lax.axis_size("tm")
    tile, channels = states.shape[1:]
    freq, depth = w_time.shape
    width = w_query.shape[2]
    count = lax.axis_size("ctx")
    rows = steps * tile
    state, noise = states[0].T, noise_draws[0].T
    final = w_final.T
    packed = (steps, tile // 2, 2 * channels)
    features = fourier_rows(plan, freq, steps)

    copies = call(pack_kernel, struct(packed, BF16), [VMEM], limit=8)(state)
    latents = lax.all_to_all(copies, "tm", 0, 0, tiled=True)
    outward = [(i, i + 1 if i % 2 else i - 1) for i in range(1, count - 1)]
    outer_latents = lax.ppermute(latents, "ctx", outward)
    into_value, into_final, tail = call(
        fold_kernel,
        [
            struct((freq + channels, 2 * width), BF16),
            struct((freq + channels, 2 * channels), BF16),
            struct((width, 2 * channels), BF16),
        ],
        [VMEM] * 5,
    )(w_embed, w_time, w_value[0], w_out[0], final)
    scratch = [
        pltpu.VMEM((rows, freq + channels), BF16),
        pltpu.VMEM((freq + channels, depth), BF16),
        pltpu.VMEM((depth, 2 * width), BF16),
        pltpu.SemaphoreType.DMA((4,)),
    ]
    block, chunk = 4 * tile, 512
    flops = 4 * rows * depth * 256
    query, own_pair = call(
        functools.partial(project_kernel, True, block, chunk),
        [struct((rows, width), BF16), struct((rows, 2 * width), BF16)],
        [VMEM, VMEM] + [ANY] * 4 + [VMEM] * 3,
        scratch,
        flops=flops,
        moved=4 * MIB,
    )(latents, features, w_embed, w_time, w_query[0], w_key[0], into_value, gain_query, gain_key)
    own_pair, outer_latents = lax.optimization_barrier((own_pair, outer_latents))
    inner_pair = lax.ppermute(own_pair, "ctx", [(i, i ^ 1) for i in range(count)])
    outer_pair = call(
        functools.partial(project_kernel, False, block, chunk),
        struct((rows, 2 * width), BF16),
        [VMEM, VMEM] + [ANY] * 4 + [VMEM],
        scratch,
        flops=flops,
        moved=4 * MIB,
    )(outer_latents, features, w_embed, w_time, w_key[0], w_value[0], gain_key)
    sent = call(
        attend_kernel,
        struct(packed, BF16),
        [SMEM] + [VMEM] * 10,
        flops=flops // 8,
        moved=4 * MIB,
    )(
        plan,
        query,
        own_pair,
        inner_pair,
        outer_pair,
        tail,
        latents,
        features,
        into_final,
        state,
        noise,
    )
    taken = lax.all_to_all(sent, "tm", 0, 0, tiled=True)
    total = call(sum_kernel, struct((channels, tile), F32), [VMEM], limit=8)(taken)
    return total.T[None]


def solution(mesh):
    return jax.shard_map(
        per_device,
        mesh=mesh,
        in_specs=(
            P("tm", "ctx", None),
            P("tm", "ctx", None),
            P(),
            P(),
            P(),
            P("tm", None, None),
            P("tm", None, None),
            P("tm", None, None),
            P("tm", None),
            P("tm", None),
            P("tm", None, None),
            P(),
        ),
        out_specs=P("tm", "ctx", None),
        check_vma=False,
    )
```

```python
import functools
import math

import jax
import jax.numpy as jnp
from jax import lax
from jax.experimental import pallas as pl
from jax.experimental.pallas import tpu as pltpu
from jax.sharding import PartitionSpec as P

F32, BF16 = jnp.float32, jnp.bfloat16
MIB = 1 << 20
FOLD_LIMIT = 54
VMEM = pl.BlockSpec(memory_space=pltpu.VMEM)
HBM = pl.BlockSpec(memory_space=pltpu.HBM)
SMEM = pl.BlockSpec(memory_space=pltpu.SMEM)
NT = (((1,), (1,)), ((), ()))


def fourier_rows(plan, freq_count, step_count):
    half_freq = freq_count // 2
    frequency = jnp.exp(-math.log(10000.0) * jnp.arange(half_freq, dtype=F32) / half_freq)
    phase_arg = plan[:step_count].astype(F32)[:, None] * frequency[None, :]
    return jnp.concatenate([jnp.cos(phase_arg), jnp.sin(phase_arg)], axis=1).astype(BF16)


def dot(a, b):
    return jnp.dot(a, b, preferred_element_type=F32)


def split(value):
    high = value.astype(BF16)
    return high, (value - high.astype(F32)).astype(BF16)


def pack_kernel(state_ref, own_ref, copies_ref):
    rows = state_ref[...].T.astype(BF16)
    half = rows.shape[0] // 2
    packed = jnp.concatenate([rows[:half], rows[half:]], axis=1)
    own_ref[...] = packed
    copies_ref[...] = jnp.broadcast_to(packed[None], copies_ref.shape)


def input_rows(packed, features):
    low = lax.broadcasted_iota(jnp.int32, packed.shape, 1) < packed.shape[1] // 2
    zero = jnp.zeros_like(packed)
    rows = jnp.concatenate([jnp.where(low, packed, zero), jnp.where(low, zero, packed)], axis=0)
    features = jnp.broadcast_to(features, (rows.shape[0], features.shape[1]))
    return jnp.concatenate([features, rows], axis=1)


def fold_kernel(
    plan_ref,
    own_ref,
    feature_ref,
    state_ref,
    noise_ref,
    embed_hbm,
    time_hbm,
    value_hbm,
    out_hbm,
    final_hbm,
    gain_query_hbm,
    gain_key_hbm,
    into_value,
    tail,
    extra_ref,
    gains,
    sizes,
    first,
    value_ref,
    out_ref,
    final_ref,
    sems,
):
    freq, width = time_hbm.shape[0], value_hbm.shape[1]
    channels = embed_hbm.shape[0]
    pairs = (
        (time_hbm, first.at[:freq]),
        (embed_hbm, first.at[freq:]),
        (value_hbm, value_ref),
        (final_hbm, final_ref),
        (out_hbm, out_ref),
        (gain_query_hbm, gains.at[0:1]),
        (gain_key_hbm, gains.at[1:2]),
    )
    copies = [pltpu.make_async_copy(a, b, sems.at[i]) for i, (a, b) in enumerate(pairs)]
    for copy in copies:
        copy.start()
    mine = lax.axis_index("tm")
    features = feature_ref[...].astype(F32)
    chosen = lax.broadcasted_iota(jnp.int32, features.shape, 0) == mine
    features = jnp.sum(jnp.where(chosen, features, 0.0), axis=0, keepdims=True).astype(BF16)
    taken = input_rows(own_ref[...], features)
    for s in range(sizes.shape[0]):
        size = (plan_ref[s] - plan_ref[s + 1]).astype(F32) / 1000.0
        sizes[s : s + 1, :] = jnp.full((1, sizes.shape[1]), size, F32)
    size = (plan_ref[mine] - plan_ref[mine + 1]).astype(F32) / 1000.0
    size = jnp.full((taken.shape[0], channels), size, F32)
    for copy in copies:
        copy.wait()
    left, final = first[...], final_ref[...]
    high, low = split(dot(left, value_ref[...]))
    into_value[:, :width] = jnp.concatenate([high, high[freq:]], axis=0)
    into_value[:, width:] = jnp.concatenate([low, low[freq:]], axis=0)
    product = lax.dot_general(left, final, NT, preferred_element_type=F32)
    product = jnp.concatenate(split(product), axis=1)
    residual = dot(taken, jnp.concatenate([product, product[freq:]], axis=0))
    residual = residual[:, :channels] + residual[:, channels:]
    state = state_ref[...].T
    rest = state - state.astype(BF16).astype(F32)
    extra = size * residual + jnp.sqrt(size) * noise_ref[...].T + jnp.where(mine == 0, rest, 0.0)
    half = extra.shape[0] // 2
    extra_ref[...] = jnp.concatenate([extra[:half], extra[half:]], axis=1)
    high, low = split(lax.dot_general(out_ref[...], final, NT, preferred_element_type=F32))
    tail[:width, :] = jnp.concatenate([high, high], axis=1)
    tail[width:, :] = jnp.concatenate([low, low], axis=1)


def rms_gain(values, gain):
    scale = lax.rsqrt(jnp.mean(values * values, axis=-1, keepdims=True) + 1e-06)
    return values * scale * gain


def project_kernel(
    own, group, chunk, latent_ref, feature_ref, time_ref, embed_ref, left_ref, right_ref, gains, *rest
):
    if own:
        into_value, query_out, pair_out = rest
    else:
        (pair_out,) = rest
    steps, half, _ = latent_ref.shape
    depth, width = left_ref.shape
    tile = 2 * half
    features = feature_ref[...].astype(F32)
    for s in range(0, steps, group):
        here = slice(s * tile, (s + group) * tile)
        taken = [
            input_rows(latent_ref[t], features[t : t + 1].astype(BF16)) for t in range(s, s + group)
        ]
        taken = jnp.concatenate(taken, axis=0)
        total = None
        for n in range(0, depth, chunk):
            part = slice(n, n + chunk)
            embed = embed_ref[:, part]
            first = jnp.concatenate([time_ref[:, part], embed, embed], axis=0)
            second = jnp.concatenate([left_ref[part, :], right_ref[part, :]], axis=1)
            product = dot(dot(taken, first).astype(BF16), second)
            total = product if total is None else total + product
        if own:
            query_out[here, :] = rms_gain(total[:, :width], gains[0:1, :]).astype(BF16)
            pair_out[here, :width] = rms_gain(total[:, width:], gains[1:2, :]).astype(BF16)
            values = dot(taken, into_value[...])
            pair_out[here, width:] = (values[:, :width] + values[:, width:]).astype(BF16)
        else:
            pair_out[here, :width] = rms_gain(total[:, :width], gains[1:2, :]).astype(BF16)
            pair_out[here, width:] = total[:, width:].astype(BF16)


def attend_kernel(
    group, query_ref, own_ref, inner_ref, outer_ref, tail_ref, extra_ref, sizes, sent_ref, scores
):
    steps, half, both = sent_ref.shape
    tile, width = 2 * half, query_ref.shape[1]
    pairs = (own_ref, inner_ref, outer_ref)
    mine, place = lax.axis_index("tm"), lax.axis_index("ctx")
    rate = math.log2(math.e) / math.sqrt(width)
    for s in range(steps):
        here = slice(s * tile, (s + 1) * tile)
        keys = jnp.concatenate([r[here, :width] for r in pairs], axis=0)
        scores[here, :] = lax.dot_general(query_ref[here, :], keys, NT, preferred_element_type=F32)

    @pl.when((place == 0) | (place == lax.axis_size("ctx") - 1))
    def _():
        scores[:, 2 * tile :] = jnp.full((steps * tile, tile), -1e30, F32)

    low = lax.broadcasted_iota(jnp.int32, (half, both), 1) < both // 2
    running, extra = jnp.zeros((half, both), F32), extra_ref[...]
    for s in range(0, steps, group):
        values = scores[s * tile : (s + group) * tile, :]
        top = jnp.max(values, axis=-1, keepdims=True)
        expo = jnp.exp2((values - top) * rate)
        probs = (expo * (1.0 / jnp.sum(expo, axis=-1, keepdims=True))).astype(BF16)
        attended = []
        for t in range(s, s + group):
            here = slice(t * tile, (t + 1) * tile)
            seen = jnp.concatenate([r[here, width:] for r in pairs], axis=0)
            attended.append(dot(probs[(t - s) * tile : (t - s + 1) * tile], seen).astype(BF16))
        attended = jnp.concatenate(attended, axis=0)
        terms = dot(jnp.concatenate([attended, attended], axis=1), tail_ref[...])
        for t in range(s, s + group):
            row = (t - s) * tile
            packed = jnp.where(low, terms[row : row + half], terms[row + half : row + tile])
            running = running + sizes[t : t + 1, :] * packed
            sent_ref[t] = (running + jnp.where(t >= mine, extra, 0.0)).astype(BF16)


def sum_kernel(taken_ref, latent_ref, out_ref):
    total = jnp.sum(taken_ref[...].astype(F32), axis=0) + latent_ref[0].astype(F32)
    channels = total.shape[1] // 2
    out_ref[...] = jnp.concatenate([total[:, :channels], total[:, channels:]], axis=0).T


def call(kernel, shapes, specs, scratch=(), limit=24, flops=0, moved=0):
    many = isinstance(shapes, (list, tuple))
    return pl.pallas_call(
        kernel,
        out_shape=shapes,
        in_specs=specs,
        out_specs=[VMEM] * len(shapes) if many else VMEM,
        scratch_shapes=list(scratch),
        compiler_params=pltpu.CompilerParams(vmem_limit_bytes=limit * MIB),
        cost_estimate=pl.CostEstimate(flops=flops, bytes_accessed=moved, transcendentals=0),
    )


def struct(shape, dtype):
    return jax.ShapeDtypeStruct(shape, dtype)


def per_device(
    states,
    noise_draws,
    plan,
    w_embed,
    w_time,
    w_query,
    w_key,
    w_value,
    gain_query,
    gain_key,
    w_out,
    w_final,
):
    steps = lax.axis_size("tm")
    tile, channels = states.shape[1:]
    freq, depth = w_time.shape
    width = w_query.shape[2]
    count = lax.axis_size("ctx")
    rows = steps * tile
    state, noise = states[0].T, noise_draws[0].T
    final = w_final.T
    packed = (steps, tile // 2, 2 * channels)
    features = fourier_rows(plan, freq, steps)

    own, copies = call(
        pack_kernel, [struct(packed[1:], BF16), struct(packed, BF16)], [VMEM], limit=8
    )(state)
    latents = lax.all_to_all(copies, "tm", 0, 0, tiled=True)
    outward = [(i, i + 1 if i % 2 else i - 1) for i in range(1, count - 1)]
    outer_latents = lax.ppermute(latents, "ctx", outward)
    inputs = freq + 2 * channels
    into_value, tail, extra, gains, sizes = call(
        fold_kernel,
        [
            struct((inputs, 2 * width), BF16),
            struct((2 * width, 2 * channels), BF16),
            struct(packed[1:], F32),
            struct((2, width), F32),
            struct((steps, 2 * channels), F32),
        ],
        [SMEM] + [VMEM] * 4 + [HBM] * 7,
        [
            pltpu.VMEM((freq + channels, depth), BF16),
            pltpu.VMEM((depth, width), BF16),
            pltpu.VMEM((width, depth), BF16),
            pltpu.VMEM((channels, depth), BF16),
            pltpu.SemaphoreType.DMA((7,)),
        ],
        limit=FOLD_LIMIT,
        flops=MIB,
        moved=1024,
    )(
        plan,
        own,
        features,
        state,
        noise,
        w_embed,
        w_time,
        w_value[0],
        w_out[0],
        final,
        gain_query,
        gain_key,
    )
    flops = 40 * rows * depth * 256
    query, own_pair = call(
        functools.partial(project_kernel, True, 4, 256),
        [struct((rows, width), BF16), struct((rows, 2 * width), BF16)],
        [VMEM] * 8,
        flops=flops,
        moved=4 * MIB,
    )(latents, features, w_time, w_embed, w_query[0], w_key[0], gains, into_value)
    inner_pair = lax.ppermute(own_pair, "ctx", [(i, i ^ 1) for i in range(count)])
    outer_pair = call(
        functools.partial(project_kernel, False, 4, 256),
        struct((rows, 2 * width), BF16),
        [VMEM] * 7,
        flops=flops,
        moved=4 * MIB,
    )(outer_latents, features, w_time, w_embed, w_key[0], w_value[0], gains)
    sent = call(
        functools.partial(attend_kernel, 4),
        struct(packed, BF16),
        [VMEM] * 7,
        [pltpu.VMEM((rows, 3 * tile), F32)],
        flops=flops // 8,
        moved=4 * MIB,
    )(query, own_pair, inner_pair, outer_pair, tail, extra, sizes)
    taken = lax.all_to_all(sent, "tm", 0, 0, tiled=True)
    total = call(sum_kernel, struct((channels, tile), F32), [VMEM] * 2, limit=8)(taken, latents)
    return total.T[None]


def solution(mesh):
    return jax.shard_map(
        per_device,
        mesh=mesh,
        in_specs=(
            P("tm", "ctx", None),
            P("tm", "ctx", None),
            P(),
            P(),
            P(),
            P("tm", None, None),
            P("tm", None, None),
            P("tm", None, None),
            P("tm", None),
            P("tm", None),
            P("tm", None, None),
            P(),
        ),
        out_specs=P("tm", "ctx", None),
        check_vma=False,
    )
```

```python
import functools
import math

import jax
import jax.numpy as jnp
from jax import lax
from jax.experimental import pallas as pl
from jax.experimental.pallas import tpu as pltpu
from jax.sharding import PartitionSpec as P

F32, BF16 = jnp.float32, jnp.bfloat16
MIB = 1 << 20
FOLD_LIMIT = 53
VMEM = pl.BlockSpec(memory_space=pltpu.VMEM)
HBM = pl.BlockSpec(memory_space=pltpu.HBM)
SMEM = pl.BlockSpec(memory_space=pltpu.SMEM)
NT = (((1,), (1,)), ((), ()))


def fourier_rows(plan, freq_count, step_count):
    half_freq = freq_count // 2
    frequency = jnp.exp(-math.log(10000.0) * jnp.arange(half_freq, dtype=F32) / half_freq)
    phase_arg = plan[:step_count].astype(F32)[:, None] * frequency[None, :]
    return jnp.concatenate([jnp.cos(phase_arg), jnp.sin(phase_arg)], axis=1).astype(BF16)


def dot(a, b):
    return jnp.dot(a, b, preferred_element_type=F32)


def split(value):
    high = value.astype(BF16)
    return high, (value - high.astype(F32)).astype(BF16)


def pack_kernel(state_ref, copies_ref):
    rows = state_ref[...].T.astype(BF16)
    half = rows.shape[0] // 2
    packed = jnp.concatenate([rows[:half], rows[half:]], axis=1)
    copies_ref[...] = jnp.broadcast_to(packed[None], copies_ref.shape)


def input_rows(packed, features):
    low = lax.broadcasted_iota(jnp.int32, packed.shape, 1) < packed.shape[1] // 2
    zero = jnp.zeros_like(packed)
    rows = jnp.concatenate([jnp.where(low, packed, zero), jnp.where(low, zero, packed)], axis=0)
    features = jnp.broadcast_to(features, (rows.shape[0], features.shape[1]))
    return jnp.concatenate([features, rows], axis=1)


def fold_kernel(
    plan_ref,
    feature_ref,
    state_ref,
    noise_ref,
    embed_hbm,
    time_hbm,
    value_hbm,
    out_hbm,
    final_hbm,
    gain_query_hbm,
    gain_key_hbm,
    into_value,
    tail,
    extra_ref,
    gains,
    sizes,
    first,
    value_ref,
    out_ref,
    final_ref,
    sems,
):
    freq, width = time_hbm.shape[0], value_hbm.shape[1]
    channels = embed_hbm.shape[0]
    pairs = (
        (time_hbm, first.at[:freq]),
        (embed_hbm, first.at[freq:]),
        (value_hbm, value_ref),
        (final_hbm, final_ref),
        (out_hbm, out_ref),
        (gain_query_hbm, gains.at[0:1]),
        (gain_key_hbm, gains.at[1:2]),
    )
    copies = [pltpu.make_async_copy(a, b, sems.at[i]) for i, (a, b) in enumerate(pairs)]
    for copy in copies:
        copy.start()
    mine = lax.axis_index("tm")
    features = feature_ref[...].astype(F32)
    chosen = lax.broadcasted_iota(jnp.int32, features.shape, 0) == mine
    features = jnp.sum(jnp.where(chosen, features, 0.0), axis=0, keepdims=True).astype(BF16)
    state = state_ref[...].T
    rows = state.astype(BF16)
    features = jnp.broadcast_to(features, (rows.shape[0], freq))
    taken = jnp.concatenate([features, rows], axis=1)
    for s in range(sizes.shape[0]):
        size = (plan_ref[s] - plan_ref[s + 1]).astype(F32) / 1000.0
        sizes[s : s + 1, :] = jnp.full((1, sizes.shape[1]), size, F32)
    size = (plan_ref[mine] - plan_ref[mine + 1]).astype(F32) / 1000.0
    size = jnp.full((taken.shape[0], channels), size, F32)
    for copy in copies:
        copy.wait()
    left, final = first[...], final_ref[...]
    high, low = split(dot(left, value_ref[...]))
    into_value[:, :width] = jnp.concatenate([high, high[freq:]], axis=0)
    into_value[:, width:] = jnp.concatenate([low, low[freq:]], axis=0)
    product = lax.dot_general(left, final, NT, preferred_element_type=F32)
    product = jnp.concatenate(split(product), axis=1)
    residual = dot(taken, product)
    residual = residual[:, :channels] + residual[:, channels:]
    rest = state - rows.astype(F32)
    extra = size * residual + jnp.sqrt(size) * noise_ref[...].T + jnp.where(mine == 0, rest, 0.0)
    half = extra.shape[0] // 2
    extra_ref[...] = jnp.concatenate([extra[:half], extra[half:]], axis=1)
    high, low = split(lax.dot_general(out_ref[...], final, NT, preferred_element_type=F32))
    tail[:width, :] = jnp.concatenate([high, high], axis=1)
    tail[width:, :] = jnp.concatenate([low, low], axis=1)


def rms_gain(values, gain):
    scale = lax.rsqrt(jnp.mean(values * values, axis=-1, keepdims=True) + 1e-06)
    return values * scale * gain


def project_kernel(
    own, group, chunk, latent_ref, feature_ref, time_ref, embed_ref, left_ref, right_ref, gains, *rest
):
    if own:
        into_value, query_out, pair_out = rest
    else:
        (pair_out,) = rest
    steps, half, _ = latent_ref.shape
    depth, width = left_ref.shape
    tile = 2 * half
    features = feature_ref[...].astype(F32)
    for s in range(0, steps, group):
        here = slice(s * tile, (s + group) * tile)
        taken = [
            input_rows(latent_ref[t], features[t : t + 1].astype(BF16)) for t in range(s, s + group)
        ]
        taken = jnp.concatenate(taken, axis=0)
        total = None
        for n in range(0, depth, chunk):
            part = slice(n, n + chunk)
            embed = embed_ref[:, part]
            first = jnp.concatenate([time_ref[:, part], embed, embed], axis=0)
            second = jnp.concatenate([left_ref[part, :], right_ref[part, :]], axis=1)
            product = dot(dot(taken, first).astype(BF16), second)
            total = product if total is None else total + product
        if own:
            query_out[here, :] = rms_gain(total[:, :width], gains[0:1, :]).astype(BF16)
            pair_out[here, :width] = rms_gain(total[:, width:], gains[1:2, :]).astype(BF16)
            values = dot(taken, into_value[...])
            pair_out[here, width:] = (values[:, :width] + values[:, width:]).astype(BF16)
        else:
            pair_out[here, :width] = rms_gain(total[:, :width], gains[1:2, :]).astype(BF16)
            pair_out[here, width:] = total[:, width:].astype(BF16)


def attend_kernel(
    group, query_ref, own_ref, inner_ref, outer_ref, tail_ref, extra_ref, sizes, sent_ref, scores
):
    steps, half, both = sent_ref.shape
    tile, width = 2 * half, query_ref.shape[1]
    pairs = (own_ref, inner_ref, outer_ref)
    mine, place = lax.axis_index("tm"), lax.axis_index("ctx")
    rate = math.log2(math.e) / math.sqrt(width)
    for s in range(steps):
        here = slice(s * tile, (s + 1) * tile)
        keys = jnp.concatenate([r[here, :width] for r in pairs], axis=0)
        scores[here, :] = lax.dot_general(query_ref[here, :], keys, NT, preferred_element_type=F32)

    @pl.when((place == 0) | (place == lax.axis_size("ctx") - 1))
    def _():
        scores[:, 2 * tile :] = jnp.full((steps * tile, tile), -1e30, F32)

    low = lax.broadcasted_iota(jnp.int32, (half, both), 1) < both // 2
    running, extra = jnp.zeros((half, both), F32), extra_ref[...]
    for s in range(0, steps, group):
        values = scores[s * tile : (s + group) * tile, :]
        top = jnp.max(values, axis=-1, keepdims=True)
        expo = jnp.exp2((values - top) * rate)
        probs = (expo * (1.0 / jnp.sum(expo, axis=-1, keepdims=True))).astype(BF16)
        attended = []
        for t in range(s, s + group):
            here = slice(t * tile, (t + 1) * tile)
            seen = jnp.concatenate([r[here, width:] for r in pairs], axis=0)
            attended.append(dot(probs[(t - s) * tile : (t - s + 1) * tile], seen).astype(BF16))
        attended = jnp.concatenate(attended, axis=0)
        terms = dot(jnp.concatenate([attended, attended], axis=1), tail_ref[...])
        for t in range(s, s + group):
            row = (t - s) * tile
            packed = jnp.where(low, terms[row : row + half], terms[row + half : row + tile])
            running = running + sizes[t : t + 1, :] * packed
            sent_ref[t] = (running + jnp.where(t >= mine, extra, 0.0)).astype(BF16)


def sum_kernel(taken_ref, latent_ref, out_ref):
    total = jnp.sum(taken_ref[...].astype(F32), axis=0) + latent_ref[0].astype(F32)
    channels = total.shape[1] // 2
    out_ref[...] = jnp.concatenate([total[:, :channels], total[:, channels:]], axis=0).T


def call(kernel, shapes, specs, scratch=(), limit=24, flops=0, moved=0):
    many = isinstance(shapes, (list, tuple))
    return pl.pallas_call(
        kernel,
        out_shape=shapes,
        in_specs=specs,
        out_specs=[VMEM] * len(shapes) if many else VMEM,
        scratch_shapes=list(scratch),
        compiler_params=pltpu.CompilerParams(vmem_limit_bytes=limit * MIB),
        cost_estimate=pl.CostEstimate(flops=flops, bytes_accessed=moved, transcendentals=0),
    )


def struct(shape, dtype):
    return jax.ShapeDtypeStruct(shape, dtype)


def per_device(
    states,
    noise_draws,
    plan,
    w_embed,
    w_time,
    w_query,
    w_key,
    w_value,
    gain_query,
    gain_key,
    w_out,
    w_final,
):
    steps = lax.axis_size("tm")
    tile, channels = states.shape[1:]
    freq, depth = w_time.shape
    width = w_query.shape[2]
    count = lax.axis_size("ctx")
    rows = steps * tile
    state, noise = states[0].T, noise_draws[0].T
    final = w_final.T
    packed = (steps, tile // 2, 2 * channels)
    features = fourier_rows(plan, freq, steps)

    copies = call(pack_kernel, struct(packed, BF16), [VMEM], limit=8)(state)
    latents = lax.all_to_all(copies, "tm", 0, 0, tiled=True)
    outward = [(i, i + 1 if i % 2 else i - 1) for i in range(1, count - 1)]
    outer_latents = lax.ppermute(latents, "ctx", outward)
    inputs = freq + 2 * channels
    into_value, tail, extra, gains, sizes = call(
        fold_kernel,
        [
            struct((inputs, 2 * width), BF16),
            struct((2 * width, 2 * channels), BF16),
            struct(packed[1:], F32),
            struct((2, width), F32),
            struct((steps, 2 * channels), F32),
        ],
        [SMEM] + [VMEM] * 3 + [HBM] * 7,
        [
            pltpu.VMEM((freq + channels, depth), BF16),
            pltpu.VMEM((depth, width), BF16),
            pltpu.VMEM((width, depth), BF16),
            pltpu.VMEM((channels, depth), BF16),
            pltpu.SemaphoreType.DMA((7,)),
        ],
        limit=FOLD_LIMIT,
        flops=MIB,
        moved=1024,
    )(
        plan,
        features,
        state,
        noise,
        w_embed,
        w_time,
        w_value[0],
        w_out[0],
        final,
        gain_query,
        gain_key,
    )
    flops = 40 * rows * depth * 256
    query, own_pair = call(
        functools.partial(project_kernel, True, 8, 256),
        [struct((rows, width), BF16), struct((rows, 2 * width), BF16)],
        [VMEM] * 8,
        flops=flops,
        moved=4 * MIB,
    )(latents, features, w_time, w_embed, w_query[0], w_key[0], gains, into_value)
    inner_pair = lax.ppermute(own_pair, "ctx", [(i, i ^ 1) for i in range(count)])
    outer_pair = call(
        functools.partial(project_kernel, False, 4, 256),
        struct((rows, 2 * width), BF16),
        [VMEM] * 7,
        flops=flops,
        moved=4 * MIB,
    )(outer_latents, features, w_time, w_embed, w_key[0], w_value[0], gains)
    sent = call(
        functools.partial(attend_kernel, 8),
        struct(packed, BF16),
        [VMEM] * 7,
        [pltpu.VMEM((rows, 3 * tile), F32)],
        flops=flops // 8,
        moved=4 * MIB,
    )(query, own_pair, inner_pair, outer_pair, tail, extra, sizes)
    taken = lax.all_to_all(sent, "tm", 0, 0, tiled=True)
    total = call(sum_kernel, struct((channels, tile), F32), [VMEM] * 2, limit=8)(taken, latents)
    return total.T[None]


def solution(mesh):
    return jax.shard_map(
        per_device,
        mesh=mesh,
        in_specs=(
            P("tm", "ctx", None),
            P("tm", "ctx", None),
            P(),
            P(),
            P(),
            P("tm", None, None),
            P("tm", None, None),
            P("tm", None, None),
            P("tm", None),
            P("tm", None),
            P("tm", None, None),
            P(),
        ),
        out_specs=P("tm", "ctx", None),
        check_vma=False,
    )
```

```python
import functools
import math

import jax
import jax.numpy as jnp
from jax import lax
from jax.experimental import pallas as pl
from jax.experimental.pallas import tpu as pltpu
from jax.sharding import PartitionSpec as P

F32, BF16 = jnp.float32, jnp.bfloat16
MIB = 1 << 20
FOLD_LIMIT = 53
VMEM = pl.BlockSpec(memory_space=pltpu.VMEM)
HBM = pl.BlockSpec(memory_space=pltpu.HBM)
SMEM = pl.BlockSpec(memory_space=pltpu.SMEM)
NT = (((1,), (1,)), ((), ()))


def fourier_rows(plan, freq_count, step_count):
    half_freq = freq_count // 2
    frequency = jnp.exp(-math.log(10000.0) * jnp.arange(half_freq, dtype=F32) / half_freq)
    phase_arg = plan[:step_count].astype(F32)[:, None] * frequency[None, :]
    return jnp.concatenate([jnp.cos(phase_arg), jnp.sin(phase_arg)], axis=1).astype(BF16)


def dot(a, b):
    return jnp.dot(a, b, preferred_element_type=F32)


def split(value):
    high = value.astype(BF16)
    return high, (value - high.astype(F32)).astype(BF16)


def pack_kernel(state_ref, copies_ref):
    rows = state_ref[...].T.astype(BF16)
    half = rows.shape[0] // 2
    packed = jnp.concatenate([rows[:half], rows[half:]], axis=1)
    copies_ref[...] = jnp.broadcast_to(packed[None], copies_ref.shape)


def input_rows(packed, features):
    low = lax.broadcasted_iota(jnp.int32, packed.shape, 1) < packed.shape[1] // 2
    zero = jnp.zeros_like(packed)
    rows = jnp.concatenate([jnp.where(low, packed, zero), jnp.where(low, zero, packed)], axis=0)
    features = jnp.broadcast_to(features, (rows.shape[0], features.shape[1]))
    return jnp.concatenate([features, rows], axis=1)


def fold_kernel(
    plan_ref,
    feature_ref,
    state_ref,
    noise_ref,
    embed_hbm,
    time_hbm,
    value_hbm,
    out_hbm,
    final_hbm,
    gain_query_hbm,
    gain_key_hbm,
    into_value,
    tail,
    extra_ref,
    gains,
    sizes,
    first,
    value_ref,
    final_ref,
    sems,
):
    freq, width = time_hbm.shape[0], value_hbm.shape[1]
    channels = embed_hbm.shape[0]
    pairs = (
        (time_hbm, first.at[:freq]),
        (embed_hbm, first.at[freq : freq + channels]),
        (value_hbm, value_ref),
        (final_hbm, final_ref),
        (out_hbm, first.at[freq + channels :]),
        (gain_query_hbm, gains.at[0:1]),
        (gain_key_hbm, gains.at[1:2]),
    )
    copies = [pltpu.make_async_copy(a, b, sems.at[i]) for i, (a, b) in enumerate(pairs)]
    for copy in copies:
        copy.start()
    mine = lax.axis_index("tm")
    features = feature_ref[...].astype(F32)
    chosen = lax.broadcasted_iota(jnp.int32, features.shape, 0) == mine
    features = jnp.sum(jnp.where(chosen, features, 0.0), axis=0, keepdims=True).astype(BF16)
    state = state_ref[...].T
    rows = state.astype(BF16)
    features = jnp.broadcast_to(features, (rows.shape[0], freq))
    taken = jnp.concatenate([features, rows], axis=1)
    for s in range(sizes.shape[0]):
        size = (plan_ref[s] - plan_ref[s + 1]).astype(F32) / 1000.0
        sizes[s : s + 1, :] = jnp.full((1, sizes.shape[1]), size, F32)
    size = (plan_ref[mine] - plan_ref[mine + 1]).astype(F32) / 1000.0
    size = jnp.full((taken.shape[0], channels), size, F32)
    both = freq + channels
    for copy in copies[:3]:
        copy.wait()
    high, low = split(dot(first[:both, :], value_ref[...]))
    into_value[:, :width] = jnp.concatenate([high, high[freq:]], axis=0)
    into_value[:, width:] = jnp.concatenate([low, low[freq:]], axis=0)
    for copy in copies[3:]:
        copy.wait()
    product = lax.dot_general(first[...], final_ref[...], NT, preferred_element_type=F32)
    high, low = split(product)
    tail[:width, :] = jnp.concatenate([high[both:], high[both:]], axis=1)
    tail[width:, :] = jnp.concatenate([low[both:], low[both:]], axis=1)
    residual = dot(taken, jnp.concatenate([high[:both], low[:both]], axis=1))
    residual = residual[:, :channels] + residual[:, channels:]
    rest = state - rows.astype(F32)
    extra = size * residual + jnp.sqrt(size) * noise_ref[...].T + jnp.where(mine == 0, rest, 0.0)
    half = extra.shape[0] // 2
    extra_ref[...] = jnp.concatenate([extra[:half], extra[half:]], axis=1)


def rms_gain(values, gain):
    scale = lax.rsqrt(jnp.mean(values * values, axis=-1, keepdims=True) + 1e-06)
    return values * scale * gain


def project_kernel(
    own, group, chunk, latent_ref, feature_ref, time_ref, embed_ref, left_ref, right_ref, gains, *rest
):
    if own:
        into_value, query_out, pair_out = rest
    else:
        (pair_out,) = rest
    steps, half, _ = latent_ref.shape
    depth, width = left_ref.shape
    tile = 2 * half
    features = feature_ref[...].astype(F32)
    for s in range(0, steps, group):
        here = slice(s * tile, (s + group) * tile)
        taken = [
            input_rows(latent_ref[t], features[t : t + 1].astype(BF16)) for t in range(s, s + group)
        ]
        taken = jnp.concatenate(taken, axis=0)
        total = None
        for n in range(0, depth, chunk):
            part = slice(n, n + chunk)
            embed = embed_ref[:, part]
            first = jnp.concatenate([time_ref[:, part], embed, embed], axis=0)
            second = jnp.concatenate([left_ref[part, :], right_ref[part, :]], axis=1)
            product = dot(dot(taken, first).astype(BF16), second)
            total = product if total is None else total + product
        if own:
            query_out[here, :] = rms_gain(total[:, :width], gains[0:1, :]).astype(BF16)
            pair_out[here, :width] = rms_gain(total[:, width:], gains[1:2, :]).astype(BF16)
            values = dot(taken, into_value[...])
            pair_out[here, width:] = (values[:, :width] + values[:, width:]).astype(BF16)
        else:
            pair_out[here, :width] = rms_gain(total[:, :width], gains[1:2, :]).astype(BF16)
            pair_out[here, width:] = total[:, width:].astype(BF16)


def attend_kernel(
    group, query_ref, own_ref, inner_ref, outer_ref, tail_ref, extra_ref, sizes, sent_ref, scores
):
    steps, half, both = sent_ref.shape
    tile, width = 2 * half, query_ref.shape[1]
    pairs = (own_ref, inner_ref, outer_ref)
    mine, place = lax.axis_index("tm"), lax.axis_index("ctx")
    rate = math.log2(math.e) / math.sqrt(width)
    for s in range(steps):
        here = slice(s * tile, (s + 1) * tile)
        keys = jnp.concatenate([r[here, :width] for r in pairs], axis=0)
        scores[here, :] = lax.dot_general(query_ref[here, :], keys, NT, preferred_element_type=F32)

    @pl.when((place == 0) | (place == lax.axis_size("ctx") - 1))
    def _():
        scores[:, 2 * tile :] = jnp.full((steps * tile, tile), -1e30, F32)

    low = lax.broadcasted_iota(jnp.int32, (half, both), 1) < both // 2
    running, extra = jnp.zeros((half, both), F32), extra_ref[...]
    for s in range(0, steps, group):
        values = scores[s * tile : (s + group) * tile, :]
        top = jnp.max(values, axis=-1, keepdims=True)
        expo = jnp.exp2((values - top) * rate)
        probs = (expo * (1.0 / jnp.sum(expo, axis=-1, keepdims=True))).astype(BF16)
        attended = []
        for t in range(s, s + group):
            here = slice(t * tile, (t + 1) * tile)
            seen = jnp.concatenate([r[here, width:] for r in pairs], axis=0)
            attended.append(dot(probs[(t - s) * tile : (t - s + 1) * tile], seen).astype(BF16))
        attended = jnp.concatenate(attended, axis=0)
        terms = dot(jnp.concatenate([attended, attended], axis=1), tail_ref[...])
        for t in range(s, s + group):
            row = (t - s) * tile
            packed = jnp.where(low, terms[row : row + half], terms[row + half : row + tile])
            running = running + sizes[t : t + 1, :] * packed
            sent_ref[t] = (running + jnp.where(t >= mine, extra, 0.0)).astype(BF16)


def sum_kernel(taken_ref, latent_ref, out_ref):
    total = jnp.sum(taken_ref[...].astype(F32), axis=0) + latent_ref[0].astype(F32)
    channels = total.shape[1] // 2
    out_ref[...] = jnp.concatenate([total[:, :channels], total[:, channels:]], axis=0).T


def call(kernel, shapes, specs, scratch=(), limit=24, flops=0, moved=0):
    many = isinstance(shapes, (list, tuple))
    return pl.pallas_call(
        kernel,
        out_shape=shapes,
        in_specs=specs,
        out_specs=[VMEM] * len(shapes) if many else VMEM,
        scratch_shapes=list(scratch),
        compiler_params=pltpu.CompilerParams(vmem_limit_bytes=limit * MIB),
        cost_estimate=pl.CostEstimate(flops=flops, bytes_accessed=moved, transcendentals=0),
    )


def struct(shape, dtype):
    return jax.ShapeDtypeStruct(shape, dtype)


def per_device(
    states,
    noise_draws,
    plan,
    w_embed,
    w_time,
    w_query,
    w_key,
    w_value,
    gain_query,
    gain_key,
    w_out,
    w_final,
):
    steps = lax.axis_size("tm")
    tile, channels = states.shape[1:]
    freq, depth = w_time.shape
    width = w_query.shape[2]
    count = lax.axis_size("ctx")
    rows = steps * tile
    state, noise = states[0].T, noise_draws[0].T
    final = w_final.T
    packed = (steps, tile // 2, 2 * channels)
    features = fourier_rows(plan, freq, steps)

    copies = call(pack_kernel, struct(packed, BF16), [VMEM], limit=8)(state)
    latents = lax.all_to_all(copies, "tm", 0, 0, tiled=True)
    outward = [(i, i + 1 if i % 2 else i - 1) for i in range(1, count - 1)]
    outer_latents = lax.ppermute(latents, "ctx", outward)
    inputs = freq + 2 * channels
    into_value, tail, extra, gains, sizes = call(
        fold_kernel,
        [
            struct((inputs, 2 * width), BF16),
            struct((2 * width, 2 * channels), BF16),
            struct(packed[1:], F32),
            struct((2, width), F32),
            struct((steps, 2 * channels), F32),
        ],
        [SMEM] + [VMEM] * 3 + [HBM] * 7,
        [
            pltpu.VMEM((freq + channels + width, depth), BF16),
            pltpu.VMEM((depth, width), BF16),
            pltpu.VMEM((channels, depth), BF16),
            pltpu.SemaphoreType.DMA((7,)),
        ],
        limit=FOLD_LIMIT,
        flops=MIB,
        moved=1024,
    )(
        plan,
        features,
        state,
        noise,
        w_embed,
        w_time,
        w_value[0],
        w_out[0],
        final,
        gain_query,
        gain_key,
    )
    flops = 40 * rows * depth * 256
    query, own_pair = call(
        functools.partial(project_kernel, True, 8, 256),
        [struct((rows, width), BF16), struct((rows, 2 * width), BF16)],
        [VMEM] * 8,
        flops=flops,
        moved=4 * MIB,
    )(latents, features, w_time, w_embed, w_query[0], w_key[0], gains, into_value)
    inner_pair = lax.ppermute(own_pair, "ctx", [(i, i ^ 1) for i in range(count)])
    outer_pair = call(
        functools.partial(project_kernel, False, 4, 256),
        struct((rows, 2 * width), BF16),
        [VMEM] * 7,
        flops=flops,
        moved=4 * MIB,
    )(outer_latents, features, w_time, w_embed, w_key[0], w_value[0], gains)
    sent = call(
        functools.partial(attend_kernel, 8),
        struct(packed, BF16),
        [VMEM] * 7,
        [pltpu.VMEM((rows, 3 * tile), F32)],
        flops=flops // 8,
        moved=4 * MIB,
    )(query, own_pair, inner_pair, outer_pair, tail, extra, sizes)
    taken = lax.all_to_all(sent, "tm", 0, 0, tiled=True)
    total = call(sum_kernel, struct((channels, tile), F32), [VMEM] * 2, limit=8)(taken, latents)
    return total.T[None]


def solution(mesh):
    return jax.shard_map(
        per_device,
        mesh=mesh,
        in_specs=(
            P("tm", "ctx", None),
            P("tm", "ctx", None),
            P(),
            P(),
            P(),
            P("tm", None, None),
            P("tm", None, None),
            P("tm", None, None),
            P("tm", None),
            P("tm", None),
            P("tm", None, None),
            P(),
        ),
        out_specs=P("tm", "ctx", None),
        check_vma=False,
    )
```

```python
import functools
import math

import jax
import jax.numpy as jnp
from jax import lax
from jax.experimental import pallas as pl
from jax.experimental.pallas import tpu as pltpu
from jax.sharding import PartitionSpec as P

F32, BF16 = jnp.float32, jnp.bfloat16
MIB = 1 << 20
FOLD_LIMIT = 53
VMEM = pl.BlockSpec(memory_space=pltpu.VMEM)
HBM = pl.BlockSpec(memory_space=pltpu.HBM)
SMEM = pl.BlockSpec(memory_space=pltpu.SMEM)
NT = (((1,), (1,)), ((), ()))


def fourier_rows(plan, freq_count, step_count):
    half_freq = freq_count // 2
    frequency = jnp.exp(-math.log(10000.0) * jnp.arange(half_freq, dtype=F32) / half_freq)
    phase_arg = plan[:step_count].astype(F32)[:, None] * frequency[None, :]
    return jnp.concatenate([jnp.cos(phase_arg), jnp.sin(phase_arg)], axis=1).astype(BF16)


def dot(a, b):
    return jnp.dot(a, b, preferred_element_type=F32)


def split(value):
    high = value.astype(BF16)
    return high, (value - high.astype(F32)).astype(BF16)


def pack_kernel(state_ref, copies_ref):
    rows = state_ref[...].T.astype(BF16)
    half = rows.shape[0] // 2
    packed = jnp.concatenate([rows[:half], rows[half:]], axis=1)
    copies_ref[...] = jnp.broadcast_to(packed[None], copies_ref.shape)


def input_rows(packed, features):
    low = lax.broadcasted_iota(jnp.int32, packed.shape, 1) < packed.shape[1] // 2
    zero = jnp.zeros_like(packed)
    rows = jnp.concatenate([jnp.where(low, packed, zero), jnp.where(low, zero, packed)], axis=0)
    features = jnp.broadcast_to(features, (rows.shape[0], features.shape[1]))
    return jnp.concatenate([features, rows], axis=1)


def fold_kernel(
    plan_ref,
    feature_ref,
    state_ref,
    noise_ref,
    embed_hbm,
    time_hbm,
    value_hbm,
    out_hbm,
    final_hbm,
    gain_query_hbm,
    gain_key_hbm,
    into_value,
    tail,
    extra_ref,
    gains,
    sizes,
    first,
    value_ref,
    final_ref,
    sems,
):
    freq, width = time_hbm.shape[0], value_hbm.shape[1]
    channels = embed_hbm.shape[0]
    pairs = (
        (time_hbm, first.at[:freq]),
        (embed_hbm, first.at[freq : freq + channels]),
        (value_hbm, value_ref),
        (final_hbm, final_ref),
        (out_hbm, first.at[freq + channels :]),
        (gain_query_hbm, gains.at[0:1]),
        (gain_key_hbm, gains.at[1:2]),
    )
    copies = [pltpu.make_async_copy(a, b, sems.at[i]) for i, (a, b) in enumerate(pairs)]
    for copy in copies:
        copy.start()
    mine = lax.axis_index("tm")
    features = feature_ref[...].astype(F32)
    chosen = lax.broadcasted_iota(jnp.int32, features.shape, 0) == mine
    features = jnp.sum(jnp.where(chosen, features, 0.0), axis=0, keepdims=True).astype(BF16)
    state = state_ref[...].T
    rows = state.astype(BF16)
    features = jnp.broadcast_to(features, (rows.shape[0], freq))
    taken = jnp.concatenate([features, rows], axis=1)
    for s in range(sizes.shape[0]):
        size = (plan_ref[s] - plan_ref[s + 1]).astype(F32) / 1000.0
        sizes[s : s + 1, :] = jnp.full((1, sizes.shape[1]), size, F32)
    size = (plan_ref[mine] - plan_ref[mine + 1]).astype(F32) / 1000.0
    size = jnp.full((taken.shape[0], channels), size, F32)
    both = freq + channels
    for copy in copies[:3]:
        copy.wait()
    high, low = split(dot(first[:both, :], value_ref[...]))
    into_value[:, :width] = jnp.concatenate([high, high[freq:]], axis=0)
    into_value[:, width:] = jnp.concatenate([low, low[freq:]], axis=0)
    for copy in copies[3:]:
        copy.wait()
    product = lax.dot_general(first[...], final_ref[...], NT, preferred_element_type=F32)
    high, low = split(product)
    tail[:width, :] = jnp.concatenate([high[both:], high[both:]], axis=1)
    tail[width:, :] = jnp.concatenate([low[both:], low[both:]], axis=1)
    residual = dot(taken, jnp.concatenate([high[:both], low[:both]], axis=1))
    residual = residual[:, :channels] + residual[:, channels:]
    rest = state - rows.astype(F32)
    extra = size * residual + jnp.sqrt(size) * noise_ref[...].T + jnp.where(mine == 0, rest, 0.0)
    half = extra.shape[0] // 2
    extra_ref[...] = jnp.concatenate([extra[:half], extra[half:]], axis=1)


def rms_gain(values, gain):
    scale = lax.rsqrt(jnp.mean(values * values, axis=-1, keepdims=True) + 1e-06)
    return values * scale * gain


def project_kernel(
    own, group, chunk, latent_ref, feature_ref, time_ref, embed_ref, left_ref, right_ref, gains, *rest
):
    if own:
        into_value, query_out, pair_out = rest
    else:
        (pair_out,) = rest
    steps, half, _ = latent_ref.shape
    depth, width = left_ref.shape
    tile = 2 * half
    features = feature_ref[...].astype(F32)
    for s in range(0, steps, group):
        here = slice(s * tile, (s + group) * tile)
        taken = [
            input_rows(latent_ref[t], features[t : t + 1].astype(BF16)) for t in range(s, s + group)
        ]
        taken = jnp.concatenate(taken, axis=0)
        total = None
        for n in range(0, depth, chunk):
            part = slice(n, n + chunk)
            embed = embed_ref[:, part]
            first = jnp.concatenate([time_ref[:, part], embed, embed], axis=0)
            second = jnp.concatenate([left_ref[part, :], right_ref[part, :]], axis=1)
            product = dot(dot(taken, first).astype(BF16), second)
            total = product if total is None else total + product
        if own:
            query_out[here, :] = rms_gain(total[:, :width], gains[0:1, :]).astype(BF16)
            pair_out[here, :width] = rms_gain(total[:, width:], gains[1:2, :]).astype(BF16)
            values = dot(taken, into_value[...])
            pair_out[here, width:] = (values[:, :width] + values[:, width:]).astype(BF16)
        else:
            pair_out[here, :width] = rms_gain(total[:, :width], gains[1:2, :]).astype(BF16)
            pair_out[here, width:] = total[:, width:].astype(BF16)


def attend_kernel(
    group, query_ref, own_ref, inner_ref, outer_ref, tail_ref, extra_ref, sizes, sent_ref, scores
):
    steps, half, both = sent_ref.shape
    tile, width = 2 * half, query_ref.shape[1]
    pairs = (own_ref, inner_ref, outer_ref)
    mine, place = lax.axis_index("tm"), lax.axis_index("ctx")
    rate = math.log2(math.e) / math.sqrt(width)
    for s in range(steps):
        here = slice(s * tile, (s + 1) * tile)
        keys = jnp.concatenate([r[here, :width] for r in pairs], axis=0)
        scores[here, :] = lax.dot_general(query_ref[here, :], keys, NT, preferred_element_type=F32)

    @pl.when((place == 0) | (place == lax.axis_size("ctx") - 1))
    def _():
        scores[:, 2 * tile :] = jnp.full((steps * tile, tile), -1e30, F32)

    low = lax.broadcasted_iota(jnp.int32, (half, both), 1) < both // 2
    running, extra = jnp.zeros((half, both), F32), extra_ref[...]
    for s in range(0, steps, group):
        values = scores[s * tile : (s + group) * tile, :]
        top = jnp.max(values, axis=-1, keepdims=True)
        expo = jnp.exp2((values - top) * rate)
        probs = (expo * (1.0 / jnp.sum(expo, axis=-1, keepdims=True))).astype(BF16)
        attended = []
        for t in range(s, s + group):
            here = slice(t * tile, (t + 1) * tile)
            seen = jnp.concatenate([r[here, width:] for r in pairs], axis=0)
            attended.append(dot(probs[(t - s) * tile : (t - s + 1) * tile], seen).astype(BF16))
        attended = jnp.concatenate(attended, axis=0)
        terms = dot(jnp.concatenate([attended, attended], axis=1), tail_ref[...])
        for t in range(s, s + group):
            row = (t - s) * tile
            packed = jnp.where(low, terms[row : row + half], terms[row + half : row + tile])
            running = running + sizes[t : t + 1, :] * packed
            sent_ref[t] = (running + jnp.where(t >= mine, extra, 0.0)).astype(BF16)


def sum_kernel(taken_ref, latent_ref, out_ref):
    total = jnp.sum(taken_ref[...].astype(F32), axis=0) + latent_ref[0].astype(F32)
    channels = total.shape[1] // 2
    out_ref[...] = jnp.concatenate([total[:, :channels], total[:, channels:]], axis=0).T


def call(kernel, shapes, specs, scratch=(), limit=24, flops=0, moved=0):
    many = isinstance(shapes, (list, tuple))
    return pl.pallas_call(
        kernel,
        out_shape=shapes,
        in_specs=specs,
        out_specs=[VMEM] * len(shapes) if many else VMEM,
        scratch_shapes=list(scratch),
        compiler_params=pltpu.CompilerParams(vmem_limit_bytes=limit * MIB),
        cost_estimate=pl.CostEstimate(flops=flops, bytes_accessed=moved, transcendentals=0),
    )


def struct(shape, dtype):
    return jax.ShapeDtypeStruct(shape, dtype)


def per_device(
    states,
    noise_draws,
    plan,
    w_embed,
    w_time,
    w_query,
    w_key,
    w_value,
    gain_query,
    gain_key,
    w_out,
    w_final,
):
    steps = lax.axis_size("tm")
    tile, channels = states.shape[1:]
    freq, depth = w_time.shape
    width = w_query.shape[2]
    count = lax.axis_size("ctx")
    rows = steps * tile
    state, noise = states[0].T, noise_draws[0].T
    final = w_final.T
    packed = (steps, tile // 2, 2 * channels)
    features = fourier_rows(plan, freq, steps)

    copies = call(pack_kernel, struct(packed, BF16), [VMEM], limit=8)(state)
    latents = lax.all_to_all(copies, "tm", 0, 0, tiled=True)
    outward = [(i, i + 1 if i % 2 else i - 1) for i in range(1, count - 1)]
    outer_latents = lax.ppermute(latents, "ctx", outward)
    inputs = freq + 2 * channels
    into_value, tail, extra, gains, sizes = call(
        fold_kernel,
        [
            struct((inputs, 2 * width), BF16),
            struct((2 * width, 2 * channels), BF16),
            struct(packed[1:], F32),
            struct((2, width), F32),
            struct((steps, 2 * channels), F32),
        ],
        [SMEM] + [VMEM] * 3 + [HBM] * 7,
        [
            pltpu.VMEM((freq + channels + width, depth), BF16),
            pltpu.VMEM((depth, width), BF16),
            pltpu.VMEM((channels, depth), BF16),
            pltpu.SemaphoreType.DMA((7,)),
        ],
        limit=FOLD_LIMIT,
        flops=MIB,
        moved=1024,
    )(
        plan,
        features,
        state,
        noise,
        w_embed,
        w_time,
        w_value[0],
        w_out[0],
        final,
        gain_query,
        gain_key,
    )
    flops = 40 * rows * depth * 256
    query, own_pair = call(
        functools.partial(project_kernel, True, 8, 256),
        [struct((rows, width), BF16), struct((rows, 2 * width), BF16)],
        [VMEM] * 8,
        flops=flops,
        moved=4 * MIB,
    )(latents, features, w_time, w_embed, w_query[0], w_key[0], gains, into_value)
    inner_pair = lax.ppermute(own_pair, "ctx", [(i, i ^ 1) for i in range(count)])
    outer_pair = call(
        functools.partial(project_kernel, False, 4, 256),
        struct((rows, 2 * width), BF16),
        [VMEM] * 7,
        flops=flops,
        moved=4 * MIB,
    )(outer_latents, features, w_time, w_embed, w_key[0], w_value[0], gains)
    sent = call(
        functools.partial(attend_kernel, 16),
        struct(packed, BF16),
        [VMEM] * 7,
        [pltpu.VMEM((rows, 3 * tile), F32)],
        flops=flops // 8,
        moved=4 * MIB,
    )(query, own_pair, inner_pair, outer_pair, tail, extra, sizes)
    taken = lax.all_to_all(sent, "tm", 0, 0, tiled=True)
    total = call(sum_kernel, struct((channels, tile), F32), [VMEM] * 2, limit=8)(taken, latents)
    return total.T[None]


def solution(mesh):
    return jax.shard_map(
        per_device,
        mesh=mesh,
        in_specs=(
            P("tm", "ctx", None),
            P("tm", "ctx", None),
            P(),
            P(),
            P(),
            P("tm", None, None),
            P("tm", None, None),
            P("tm", None, None),
            P("tm", None),
            P("tm", None),
            P("tm", None, None),
            P(),
        ),
        out_specs=P("tm", "ctx", None),
        check_vma=False,
    )
```
